128 devices in a mesh: gx: 4 (over y), gy: 32 (over x, z, core).
Axes of the slice: x: 4, y: 4, z: 4, core: 2. Of those that a mesh axis runs over, the one named last changes fastest.
Arguments:
- multipoles_fine: bfloat16 [121, 131072], P(None, ('gx', 'gy')), may hold values from -6 to 6
- multipoles_coarse: bfloat16 [121, 16384], P(None, ('gx', 'gy')), may hold values from -6 to 6
- translations: bfloat16 [316, 121, 121], replicated, may hold values from -0.046875 to 0.046875
- shift_down: float32 [8, 121, 121], replicated, may hold values from -0.5 to 0.5
- send_fine: int32 [128, 128, 64], P(('gx', 'gy')), may hold values from 0 to 1024, as said below
- send_coarse: int32 [128, 128, 16], P(('gx', 'gy')), may hold values from 0 to 128, as said below
- near_fine: int32 [316, 131072], P(None, ('gx', 'gy')), may hold values from 0 to 9216, as said below
- near_coarse: int32 [316, 16384], P(None, ('gx', 'gy')), may hold values from 0 to 2176, as said below
- parent_fine: int32 [131072], P(('gx', 'gy')), may hold values from 0 to 129, as said below
- octant_fine: int32 [131072], P(('gx', 'gy')), may hold values from 0 to 7
- counts_coarse: int32 [128], P(('gx', 'gy')), may hold values from 1 to 128, as said below
Outputs:
- local_fine: float32 [121, 131072], P(None, ('gx', 'gy'))
- local_coarse: float32 [121, 16384], P(None, ('gx', 'gy'))
The draws below stay inside these ranges and needn't reach their ends.
Inputs may be any that keep to these rules, and one draw needn't show every extreme that they name: `send_fine`: owner p's list for peer d names live level-6 slots of p first and holds 1024 (nothing) after them; no device lists boxes for itself; some owner fills all 64 entries for some peer. `send_coarse`: owner p's list for peer d names live level-5 slots of p first and holds 128 (nothing) after them; no device lists boxes for itself; some owner fills all 16 entries for some peer. `near_fine`: entries below 1024 name live own boxes, entries from 1024 on name imported columns that carry a box, and 9216 means no source; slots of boxes that are not live hold only that value. `near_coarse`: entries below 128 name live own boxes, entries from 128 on name imported columns that carry a box, and 2176 means no source; slots of boxes that are not live hold only that value. `parent_fine`: values below 128 are own live level-5 slots; 128 is the previous device's last live level-5 box and stands only in the first seven or fewer slots of a device other than the first; 129 marks a slot that is not live. `counts_coarse`: some device holds 128 live level-5 boxes.
All inputs are finite; a program needn't handle non-finite values.
Results may differ from the reference program's by a relative error of at most 0.0003.
Values may be sent and summed in bfloat16 or wider, within the bound.
No kernel may reach another device: no remote copies, remote signals or barrier semaphores. Data moves between devices by JAX's collectives and lax.ppermute only.
A program may use at most 128 MiB of HBM per device.

```python
import jax
import jax.numpy as jnp
from jax import lax

COEFFS = 121
CLASSES = 316
BOX_FINE = 1024
SEND_FINE = 64
BOX_COARSE = 128
SEND_COARSE = 16
N_GX = 4
N_GY = 32
DEVICES = 128


def layout(key):
    devices = N_GX * N_GY
    keys = jax.random.split(key, 6)
    order = jax.random.permutation(keys[0], devices)
    count_fine = jax.random.randint(keys[1], (devices,), BOX_FINE // 2, BOX_FINE + 1)
    count_fine = count_fine.at[order[0]].set(BOX_FINE).at[order[1]].set(BOX_FINE // 2)
    spill = jax.random.randint(keys[2], (devices,), 0, 8)
    spill = spill.at[0].set(0).at[order[0]].set(0)
    count_coarse = (count_fine - spill + 7) // 8
    density = jax.random.randint(keys[3], (devices,), 1, 5)
    owners = jnp.arange(devices, dtype=jnp.int32)
    distance = jnp.abs(owners[:, None] - owners[None, :])
    raw_fine = jax.random.randint(keys[4], (devices, devices), 0, SEND_FINE + 1)
    sent_fine = raw_fine * density[None, :] // 4
    sent_fine = jnp.where(distance == 1, SEND_FINE, sent_fine)
    sent_fine = jnp.where(distance == 0, 0, sent_fine)
    raw_coarse = jax.random.randint(keys[5], (devices, devices), 0, SEND_COARSE + 1)
    sent_coarse = raw_coarse * density[None, :] // 4
    sent_coarse = jnp.where(distance == 1, SEND_COARSE, sent_coarse)
    sent_coarse = jnp.where(distance == 0, 0, sent_coarse)
    return (count_fine, spill, count_coarse, sent_fine, sent_coarse)


def send_lists(key, counts, sent, width, box_count):
    devices = N_GX * N_GY
    slots = jax.random.randint(key, (devices, devices, width), 0, 1 << 20) % counts[:, None, None]
    position = jnp.arange(width, dtype=jnp.int32)
    live = position[None, None, :] < sent[:, :, None]
    return jnp.where(live, slots, box_count).astype(jnp.int32)


def near_lists(key, counts, sent, width, box_count):
    devices = N_GX * N_GY
    keys = jax.random.split(key, 4)
    shape = (CLASSES, devices, box_count)
    present = jax.random.randint(keys[0], shape, 0, 5) < 3
    target = jnp.arange(box_count, dtype=jnp.int32)[None, None, :]
    live_target = target < counts[None, :, None]
    local_source = jax.random.randint(keys[1], shape, 0, 1 << 20) % counts[None, :, None]
    column = jax.random.randint(keys[2], shape, 0, devices * width)
    owner = column // width
    place = column % width
    receiver = jnp.broadcast_to(jnp.arange(devices, dtype=jnp.int32)[None, :, None], shape)
    live_column = place < sent[owner, receiver]
    use_import = (jax.random.randint(keys[3], shape, 0, 5) < 2) & live_column
    source = jnp.where(use_import, box_count + column, local_source)
    source = jnp.where(present & live_target, source, box_count + devices * width)
    return source.reshape(CLASSES, devices * box_count).astype(jnp.int32)


def draw_send_fine(key, part):
    count_fine, spill, count_coarse, sent_fine, sent_coarse = layout(key)
    key = jax.random.fold_in(key, 11)
    return send_lists(key, count_fine, sent_fine, SEND_FINE, BOX_FINE)


def draw_send_coarse(key, part):
    count_fine, spill, count_coarse, sent_fine, sent_coarse = layout(key)
    key = jax.random.fold_in(key, 12)
    return send_lists(key, count_coarse, sent_coarse, SEND_COARSE, BOX_COARSE)


def draw_near_fine(key, part):
    count_fine, spill, count_coarse, sent_fine, sent_coarse = layout(key)
    key = jax.random.fold_in(key, 13)
    return near_lists(key, count_fine, sent_fine, SEND_FINE, BOX_FINE)


def draw_near_coarse(key, part):
    count_fine, spill, count_coarse, sent_fine, sent_coarse = layout(key)
    key = jax.random.fold_in(key, 14)
    return near_lists(key, count_coarse, sent_coarse, SEND_COARSE, BOX_COARSE)


def draw_parent_fine(key, part):
    count_fine, spill, count_coarse, sent_fine, sent_coarse = layout(key)
    devices = N_GX * N_GY
    target = jnp.arange(BOX_FINE, dtype=jnp.int32)[None, :]
    parent = (target - spill[:, None]) // 8
    parent = jnp.where(target < spill[:, None], BOX_COARSE, parent)
    parent = jnp.where(target < count_fine[:, None], parent, BOX_COARSE + 1)
    return parent.reshape(devices * BOX_FINE).astype(jnp.int32)


def draw_octant_fine(key, part):
    count_fine, spill, count_coarse, sent_fine, sent_coarse = layout(key)
    devices = N_GX * N_GY
    target = jnp.arange(BOX_FINE, dtype=jnp.int32)[None, :]
    octant = (target - spill[:, None]) % 8
    return octant.reshape(devices * BOX_FINE).astype(jnp.int32)


def draw_counts_coarse(key, part):
    count_fine, spill, count_coarse, sent_fine, sent_coarse = layout(key)
    return count_coarse.astype(jnp.int32)


def steps_of(stream_key, dims, shards, least, high):
    def one(dim, shards_of):
        steps = jax.random.uniform(jax.random.fold_in(jax.random.fold_in(stream_key, 6), dim), (shards_of,), jnp.float32, least / len(shards), high / len(shards))
        return jnp.repeat(jnp.exp(steps), dims[dim] // shards_of).reshape((-1,) + (1,) * (len(dims) - dim - 1))

    level = one(*shards[0])
    for cut in shards[1:]:
        level = level * one(*cut)
    return level


def noise(key, dims, spread, bound, pieces=(), kind=jnp.bfloat16):
    result = jax.random.normal(key, dims, jnp.float32) * spread
    if len(pieces) > 0:
        result = steps_of(key, dims, pieces, -0.22, 0.18) * result
    return jnp.clip(result, min=-bound, max=bound).astype(kind)


def setup_inputs(seed: int = 0) -> dict:
    streams_of = jax.random.split(jax.random.key(seed), 12)
    multipoles_fine = noise(streams_of[0], (COEFFS, DEVICES * BOX_FINE), 1.0, 6.0, ((1, 128),))
    multipoles_coarse = noise(streams_of[1], (COEFFS, DEVICES * BOX_COARSE), 1.0, 6.0, ((1, 128),))
    translations = noise(streams_of[2], (CLASSES, COEFFS, COEFFS), (COEFFS * CLASSES // 2) ** -0.5, 0.046875)
    shift_down = noise(streams_of[3], (8, COEFFS, COEFFS), COEFFS ** -0.5, 0.5, (), jnp.float32)
    send_fine = draw_send_fine(jax.random.fold_in(streams_of[11], 71), 0)
    send_coarse = draw_send_coarse(jax.random.fold_in(streams_of[11], 71), 0)
    near_fine = draw_near_fine(jax.random.fold_in(streams_of[11], 71), 0)
    near_coarse = draw_near_coarse(jax.random.fold_in(streams_of[11], 71), 0)
    parent_fine = draw_parent_fine(jax.random.fold_in(streams_of[11], 71), 0)
    octant_fine = draw_octant_fine(jax.random.fold_in(streams_of[11], 71), 0)
    counts_coarse = draw_counts_coarse(jax.random.fold_in(streams_of[11], 71), 0)
    return {"multipoles_fine": multipoles_fine, "multipoles_coarse": multipoles_coarse, "translations": translations, "shift_down": shift_down, "send_fine": send_fine, "send_coarse": send_coarse, "near_fine": near_fine, "near_coarse": near_coarse, "parent_fine": parent_fine, "octant_fine": octant_fine, "counts_coarse": counts_coarse}


def translate(trans_wide, table, near_rows):
    gathered = jnp.take(table, near_rows, axis=1).astype(jnp.float32)
    return jnp.einsum("cik,kcb->ib", trans_wide, gathered, precision=lax.Precision.HIGHEST)


def imports(padded, peer_lists, device, box_count):
    devices = N_GX * N_GY
    lists_here = jnp.take(peer_lists, device, axis=1).astype(jnp.int32)
    owners = jnp.arange(devices, dtype=jnp.int32)[:, None]
    columns = jnp.where(lists_here < box_count, owners * box_count + lists_here, devices * box_count).astype(jnp.int32)
    return jnp.take(padded, columns.reshape(-1), axis=1)


def level_table(multipoles, imported, device, box_count):
    own_cols = lax.dynamic_slice_in_dim(multipoles, (device * box_count).astype(jnp.int32), box_count, 1)
    zero_col = jnp.zeros((multipoles.shape[0], 1), multipoles.dtype)
    return jnp.concatenate([own_cols, imported, zero_col], axis=1)


def reference(multipoles_fine, multipoles_coarse, translations, shift_down, send_fine, send_coarse, near_fine, near_coarse, parent_fine, octant_fine, counts_coarse):
    devices = N_GX * N_GY
    coeffs = multipoles_fine.shape[0]
    trans_wide = translations.astype(jnp.float32)
    zero_col = jnp.zeros((coeffs, 1), multipoles_fine.dtype)
    padded_fine = jnp.concatenate([multipoles_fine, zero_col], axis=1)
    padded_coarse = jnp.concatenate([multipoles_coarse, zero_col], axis=1)

    def per_device(device):
        table_fine = level_table(multipoles_fine, imports(padded_fine, send_fine, device, BOX_FINE), device, BOX_FINE)
        rows_fine = lax.dynamic_slice_in_dim(near_fine, (device * BOX_FINE).astype(jnp.int32), BOX_FINE, 1)
        far_fine = translate(trans_wide, table_fine, rows_fine)
        table_coarse = level_table(multipoles_coarse, imports(padded_coarse, send_coarse, device, BOX_COARSE), device, BOX_COARSE)
        rows_coarse = lax.dynamic_slice_in_dim(near_coarse, (device * BOX_COARSE).astype(jnp.int32), BOX_COARSE, 1)
        local_here = translate(trans_wide, table_coarse, rows_coarse)
        return far_fine, local_here

    far_all, coarse_all = lax.map(per_device, jnp.arange(devices, dtype=jnp.int32))
    last_slot = (counts_coarse - 1).astype(jnp.int32)
    last_local = jnp.take_along_axis(coarse_all, jnp.broadcast_to(last_slot[:, None, None], (devices, coeffs, 1)), axis=2)[:, :, 0]
    boundary = jnp.concatenate([jnp.zeros((1, coeffs), coarse_all.dtype), last_local[:-1]], axis=0)
    parents = jnp.concatenate([coarse_all, boundary[:, :, None], jnp.zeros((devices, coeffs, 1), coarse_all.dtype)], axis=2)
    down_all = jnp.einsum("oik,nkb->niob", shift_down, parents, precision=lax.Precision.HIGHEST)
    down_all = down_all.reshape(devices, coeffs, 8 * (BOX_COARSE + 2))
    pick_codes = (octant_fine * (BOX_COARSE + 2) + parent_fine).astype(jnp.int32).reshape(devices, 1, BOX_FINE)
    picked = jnp.take_along_axis(down_all, jnp.broadcast_to(pick_codes, (devices, coeffs, BOX_FINE)), axis=2)
    local_fine = (far_all + picked).transpose(1, 0, 2).reshape(coeffs, devices * BOX_FINE)
    local_coarse = coarse_all.transpose(1, 0, 2).reshape(coeffs, devices * BOX_COARSE)
    return (local_fine, local_coarse)
```

```python
import functools

import jax
import jax.numpy as jnp
from jax import lax
from jax.experimental import pallas as pl
from jax.experimental.pallas import tpu as pltpu
from jax.sharding import PartitionSpec as P

LANES = 128
PIECE = 1024
COARSE_GROUP = 32
FINE_GROUP = 4
AXES = ("gx", "gy")


def pick_tile(table, index_of, masks):
    tile = None
    for k in range(8):
        row = jnp.broadcast_to(table[pl.ds(index_of(k), 1), :], (8, LANES))
        tile = row if tile is None else jnp.where(masks[k], row, tile)
    return tile


def translate_kernel(*refs, pieces, group, last_classes, with_down, block=256):
    piece_count = len(pieces)
    if with_down:
        near, own, imported, weights, codes, down = refs[:6]
        refs = refs[6:]
    else:
        near, own, imported, weights = refs[:4]
        refs = refs[4:]
    out, table, gathered, total, spread, right, sems = refs[:7]
    buffers = refs[7:]
    step = pl.program_id(0)
    steps = pl.num_programs(0)
    own_count = own.shape[0]
    import_count = imported.shape[0]
    boxes = total.shape[0]
    coeffs, held, _ = weights.shape
    sublane = lax.broadcasted_iota(jnp.int32, (8, LANES), 0)
    masks = [sublane == k for k in range(8)]

    def fetch(at_step, part):
        return pltpu.make_async_copy(
            near.at[at_step * piece_count + part], buffers[part], sems.at[part]
        )

    @pl.when(step == 0)
    def _():
        for part in range(piece_count):
            fetch(0, part).start()
        gathered[...] = jnp.zeros_like(gathered)
        spread[...] = jnp.zeros_like(spread)
        table[0:own_count, :] = own[...].astype(jnp.float32)

        def widen(i, carry):
            first = pl.multiple_of(i * 128, 128)
            table[pl.ds(own_count + first, 128), :] = imported[pl.ds(first, 128), :].astype(
                jnp.float32
            )
            return carry

        lax.fori_loop(0, import_count // 128, widen, 0)
        table[own_count + import_count :, :] = jnp.zeros((8, LANES), jnp.float32)
        if with_down:

            def start_rows(i, carry):
                first = pl.multiple_of(i * 8, 8)
                total[pl.ds(first, 8), :] = pick_tile(down, lambda k: codes[first + k], masks)
                return carry

            lax.fori_loop(0, boxes // 8, start_rows, 0)
        else:
            total[...] = jnp.zeros_like(total)

    offset = lax.rem(step, held // group) * group

    def widen_matrices(first, count):
        spread[first * held : (first + count) * held, 0:coeffs] = (
            weights[first : first + count].astype(jnp.float32).reshape(count * held, coeffs)
        )

    def arrange(c):
        rows = spread[pl.ds(offset + c, LANES, stride=held), :]
        right[:, c * LANES : (c + 1) * LANES] = rows.astype(jnp.bfloat16)

    def multiply(first_row, rows, first_class, classes):
        span = pl.ds(first_class * LANES, classes * LANES)
        total[first_row : first_row + rows, :] += lax.dot_general(
            gathered[first_row : first_row + rows, span],
            right[:, span],
            (((1,), (1,)), ((), ())),
            preferred_element_type=jnp.float32,
        )

    for part, (first_class, classes, first_ready, ready, spreads, arranged) in enumerate(pieces):
        extra = []
        if spreads:
            chunk = 4 if held > 8 else 8
            for first in range(0, coeffs, chunk):
                extra.append(
                    functools.partial(widen_matrices, first, min(chunk, coeffs - first))
                )
        for c in arranged:
            extra.append(functools.partial(arrange, c))
        tiles = classes * boxes // 16
        every = max(1, tiles // (len(extra) + 1))
        fetch(step, part).wait()
        buffer = buffers[part]
        done = 0
        for r in range(0, boxes, block):
            if ready:
                multiply(r, min(block, boxes), first_ready, ready)
            for c in range(classes):
                for v in range(r, min(r + block, boxes), 16):
                    halves = [
                        pick_tile(table, lambda k, at=c * boxes + v + h: buffer[at + k], masks)
                        for h in (0, 8)
                    ]
                    gathered[
                        v : v + 16, (first_class + c) * LANES : (first_class + c + 1) * LANES
                    ] = jnp.concatenate(halves, axis=0).astype(jnp.bfloat16)
                    done += 1
                    if extra and done % every == 0:
                        extra.pop(0)()
        for rest in extra:
            rest()
        fetch(jnp.minimum(step + 1, steps - 1), part).start()

    @pl.when(step == steps - 1)
    def _():
        for part in range(piece_count):
            fetch(step, part).wait()
        for r in range(0, boxes, 128):
            multiply(r, 128, 0, last_classes)
        out[...] = total[...].T[:coeffs, :]


def translate(translations, near, own, imported, pieces, group, held, class_count, down=None):
    coeffs = translations.shape[2]
    steps = near.shape[0] // len(pieces)
    boxes = PIECE // pieces[0][1]
    shared = held // group
    whole = lambda t: (0, 0)
    in_specs = [
        pl.BlockSpec(memory_space=pl.ANY),
        pl.BlockSpec(own.shape, whole),
        pl.BlockSpec(imported.shape, whole),
        pl.BlockSpec((coeffs, held, coeffs), lambda t: (0, t // shared, 0)),
    ]
    args = [near, own, imported, translations]
    if down is not None:
        in_specs += [pl.BlockSpec(memory_space=pltpu.SMEM), pl.BlockSpec(down[1].shape, whole)]
        args += list(down)
    entries = steps * len(pieces) * PIECE
    return pl.pallas_call(
        functools.partial(
            translate_kernel,
            pieces=pieces,
            group=group,
            last_classes=class_count - (steps - 1) * group,
            with_down=down is not None,
        ),
        grid=(steps,),
        in_specs=in_specs,
        out_specs=pl.BlockSpec((coeffs, boxes), whole),
        out_shape=jax.ShapeDtypeStruct((coeffs, boxes), jnp.float32),
        scratch_shapes=[
            pltpu.VMEM((own.shape[0] + imported.shape[0] + 8, LANES), jnp.float32),
            pltpu.VMEM((boxes, group * LANES), jnp.bfloat16),
            pltpu.VMEM((boxes, LANES), jnp.float32),
            pltpu.VMEM((LANES * held, LANES), jnp.float32),
            pltpu.VMEM((LANES, group * LANES), jnp.bfloat16),
            pltpu.SemaphoreType.DMA((len(pieces),)),
        ]
        + [pltpu.SMEM((PIECE,), jnp.int32) for _ in pieces],
        compiler_params=pltpu.CompilerParams(vmem_limit_bytes=48 * 2**20),
        cost_estimate=pl.CostEstimate(
            flops=2 * entries * LANES * LANES, bytes_accessed=entries * 1024, transcendentals=0
        ),
    )(*args)


def coarse_call(translations, near, own, imported):
    class_count, boxes = near.shape
    more = -class_count % COARSE_GROUP
    no_source = own.shape[0] + imported.shape[0]
    near = jnp.pad(near, ((0, more), (0, 0)), constant_values=no_source)
    share = PIECE // boxes
    pieces = tuple(
        (c, share, c, share, c == 0, range(c, c + share)) for c in range(0, COARSE_GROUP, share)
    )
    return translate(
        translations, near.reshape(-1, PIECE), own, imported, pieces, COARSE_GROUP,
        COARSE_GROUP, class_count,
    )


def fine_call(translations, near, own, imported, down):
    pieces = tuple(
        (c, 1, 0, 0 if c else FINE_GROUP, c == 1, range(2 * c - 4, 2 * c - 2) if c > 1 else ())
        for c in range(FINE_GROUP)
    )
    return translate(
        translations, near, own, imported, pieces, FINE_GROUP, 2 * FINE_GROUP, near.shape[0],
        down=down,
    )


def pack(own_rows, slots):
    places = lax.broadcasted_iota(jnp.int32, (slots.size, own_rows.shape[0]), 1)
    chosen = (slots.reshape(-1, 1) == places).astype(jnp.bfloat16)
    return jnp.dot(chosen, own_rows, preferred_element_type=jnp.float32).astype(jnp.bfloat16)


def on_device(
    multipoles_fine,
    multipoles_coarse,
    translations,
    shift_down,
    send_fine,
    send_coarse,
    near_fine,
    near_coarse,
    parent_fine,
    octant_fine,
    counts_coarse,
):
    coeffs, fine_boxes = multipoles_fine.shape
    coarse_boxes = multipoles_coarse.shape[1]
    extra = LANES - coeffs
    devices = send_fine.shape[1]

    own_coarse = jnp.pad(multipoles_coarse.T, ((0, 0), (0, extra)))
    own_fine = jnp.pad(multipoles_fine.T, ((0, 0), (0, extra)))

    def exchange(rows):
        return lax.all_to_all(rows, AXES, split_axis=0, concat_axis=0, tiled=True)

    imported_coarse = exchange(pack(own_coarse, send_coarse[0]))
    imported_fine = exchange(pack(own_fine, send_fine[0]))

    by_row = translations.transpose(1, 0, 2)
    local_coarse = coarse_call(by_row, near_coarse, own_coarse, imported_coarse)

    last_local = lax.dynamic_slice_in_dim(local_coarse, counts_coarse[0] - 1, 1, 1)
    route = [(i, i + 1) for i in range(devices - 1)]
    boundary = lax.ppermute(last_local, AXES, route)
    parents = jnp.concatenate(
        [local_coarse, boundary, jnp.zeros((coeffs, 1), jnp.float32)], axis=1
    )
    down_rows = jnp.einsum("oik,kb->obi", shift_down, parents, precision=lax.Precision.HIGHEST)
    down_rows = down_rows.reshape(8 * (coarse_boxes + 2), coeffs)
    down_rows = jnp.pad(down_rows, ((0, 0), (0, extra)))
    codes = octant_fine * (coarse_boxes + 2) + parent_fine

    local_fine = fine_call(by_row, near_fine, own_fine, imported_fine, (codes, down_rows))
    return (local_fine, local_coarse)


def solution(mesh):
    in_specs = (
        P(None, AXES),
        P(None, AXES),
        P(),
        P(),
        P(AXES, None, None),
        P(AXES, None, None),
        P(None, AXES),
        P(None, AXES),
        P(AXES),
        P(AXES),
        P(AXES),
    )
    out_specs = (P(None, AXES), P(None, AXES))
    return jax.shard_map(
        on_device, mesh=mesh, in_specs=in_specs, out_specs=out_specs, check_vma=False
    )
```

```python
import functools

import jax
import jax.numpy as jnp
from jax import lax
from jax.experimental import pallas as pl
from jax.experimental.pallas import tpu as pltpu
from jax.sharding import PartitionSpec as P

LANES = 128
PIECE = 1024
COARSE_GROUP = 32
FINE_GROUP = 4
AXES = ("gx", "gy")


def pick_tile(table, index_of, masks):
    tile = None
    for k in range(8):
        row = jnp.broadcast_to(table[pl.ds(index_of(k), 1), :], (8, LANES))
        tile = row if tile is None else jnp.where(masks[k], row, tile)
    return tile


def translate_kernel(*refs, pieces, group, last_classes, coarse, block=256):
    piece_count = len(pieces)
    near, own, imported, weights = refs[:4]
    if coarse:
        shift, out, down = refs[4:7]
    else:
        codes, down, out = refs[4:7]
    refs = refs[7:]
    table, gathered, total, spread, right, sems = refs[:6]
    buffers = refs[6:]
    step = pl.program_id(0)
    steps = pl.num_programs(0)
    own_count = own.shape[0]
    import_count = table.shape[0] - own_count - 8
    boxes = total.shape[0]
    coeffs, held, _ = weights.shape
    sublane = lax.broadcasted_iota(jnp.int32, (8, LANES), 0)
    masks = [sublane == k for k in range(8)]

    def fetch(at_step, part):
        return pltpu.make_async_copy(
            near.at[at_step * piece_count + part], buffers[part], sems.at[part]
        )

    @pl.when(step == 0)
    def _():
        for part in range(piece_count):
            fetch(0, part).start()
        gathered[...] = jnp.zeros_like(gathered)
        spread[...] = jnp.zeros_like(spread)
        right[...] = jnp.zeros_like(right)
        table[0:own_count, :] = own[...].astype(jnp.float32)

        table[own_count + import_count :, :] = jnp.zeros((8, LANES), jnp.float32)

        def widen(i, carry):
            first = pl.multiple_of(i * 128, 128)
            table[pl.ds(own_count + first, 128), :] = imported[pl.ds(first, 128), :].astype(
                jnp.float32
            )
            return carry

        lax.fori_loop(0, import_count // 128, widen, 0, unroll=2)
        if coarse:
            total[...] = jnp.zeros_like(total)
        else:

            def start_rows(i, carry):
                first = pl.multiple_of(i * 8, 8)
                total[pl.ds(first, 8), :] = pick_tile(down, lambda k: codes[first + k], masks)
                return carry

            lax.fori_loop(0, boxes // 8, start_rows, 0)

    offset = lax.rem(step, held // group) * group if held > group else 0

    def widen_matrices(source, first, count, classes):
        spread[first * 8 : (first + count) * 8, 0:coeffs] = (
            source[first : first + count, classes, :]
            .astype(jnp.float32)
            .reshape(count * 8, coeffs)
        )

    def arrange(c):
        rows = spread[pl.ds(offset + c % 8, LANES, stride=8), :]
        right[:, c * LANES : (c + 1) * LANES] = rows.astype(jnp.bfloat16)

    def multiply(first_row, rows, first_class, classes):
        span = pl.ds(first_class * LANES, classes * LANES)
        total[first_row : first_row + rows, :] += lax.dot_general(
            gathered[first_row : first_row + rows, span],
            right[:, span],
            (((1,), (1,)), ((), ())),
            preferred_element_type=jnp.float32,
        )

    for part, (first_class, classes, first_ready, ready, widened, arranged) in enumerate(pieces):
        extra = []
        if widened is not None:
            for first in range(0, coeffs, 8):
                extra.append(
                    functools.partial(
                        widen_matrices, weights, first, min(8, coeffs - first),
                        slice(widened, widened + 8),
                    )
                )
        for c in arranged:
            extra.append(functools.partial(arrange, c))
        tiles = classes * boxes // 16
        every = max(1, tiles // (len(extra) + 1))
        fetch(step, part).wait()
        buffer = buffers[part]
        done = 0
        for r in range(0, boxes, block):
            if ready:
                multiply(r, min(block, boxes), first_ready, ready)
            for c in range(classes):
                for v in range(r, min(r + block, boxes), 16):
                    halves = [
                        pick_tile(table, lambda k, at=c * boxes + v + h: buffer[at + k], masks)
                        for h in (0, 8)
                    ]
                    gathered[
                        v : v + 16, (first_class + c) * LANES : (first_class + c + 1) * LANES
                    ] = jnp.concatenate(halves, axis=0).astype(jnp.bfloat16)
                    done += 1
                    if extra and done % every == 0:
                        extra.pop(0)()
        for rest in extra:
            rest()
        fetch(jnp.minimum(step + 1, steps - 1), part).start()

    @pl.when(step == steps - 1)
    def _():
        for part in range(piece_count):
            fetch(step, part).wait()
        for r in range(0, boxes, 128):
            multiply(r, 128, 0, last_classes)
        out[...] = total[...].T[:coeffs, :]
        if coarse:
            widen_matrices(shift, 0, coeffs, slice(0, 8))
            for octant in range(8):
                down[octant * boxes : (octant + 1) * boxes, :] = lax.dot_general(
                    total[...],
                    spread[pl.ds(octant, LANES, stride=8), :],
                    (((1,), (1,)), ((), ())),
                    precision=lax.Precision.HIGHEST,
                    preferred_element_type=jnp.float32,
                )
            down[8 * boxes :, :] = jnp.zeros((8, LANES), jnp.float32)


def translate(translations, near, own, imported, more_args, pieces, group, class_count, coarse):
    coeffs = translations.shape[2]
    steps = near.shape[0] // len(pieces)
    boxes = PIECE // pieces[0][1]
    held = max(group, 8)
    shared = held // group
    whole = lambda t: (0, 0)
    in_specs = [
        pl.BlockSpec(near.shape, whole),
        pl.BlockSpec(own.shape, whole),
        pl.BlockSpec(imported.shape, whole),
        pl.BlockSpec((coeffs, held, coeffs), lambda t: (0, t // shared, 0)),
    ]
    out_specs = [pl.BlockSpec((coeffs, boxes), whole)]
    out_shape = [jax.ShapeDtypeStruct((coeffs, boxes), jnp.float32)]
    if coarse:
        in_specs.append(pl.BlockSpec(more_args[0].shape, lambda t: (0, 0, 0)))
        out_specs.append(pl.BlockSpec((8 * boxes + 8, LANES), whole))
        out_shape.append(jax.ShapeDtypeStruct((8 * boxes + 8, LANES), jnp.float32))
    else:
        in_specs.append(pl.BlockSpec(memory_space=pltpu.SMEM))
        in_specs.append(pl.BlockSpec(more_args[1].shape, whole))
    entries = steps * len(pieces) * PIECE
    return pl.pallas_call(
        functools.partial(
            translate_kernel,
            pieces=pieces,
            group=group,
            last_classes=class_count - (steps - 1) * group,
            coarse=coarse,
        ),
        grid=(steps,),
        in_specs=in_specs,
        out_specs=out_specs,
        out_shape=out_shape,
        scratch_shapes=[
            pltpu.VMEM((own.shape[0] + imported.shape[0] + 8, LANES), jnp.float32),
            pltpu.VMEM((boxes, group * LANES), jnp.bfloat16),
            pltpu.VMEM((boxes, LANES), jnp.float32),
            pltpu.VMEM((LANES * 8, LANES), jnp.float32),
            pltpu.VMEM((LANES, group * LANES), jnp.bfloat16),
            pltpu.SemaphoreType.DMA((len(pieces),)),
        ]
        + [pltpu.SMEM((PIECE,), jnp.int32) for _ in pieces],
        compiler_params=pltpu.CompilerParams(vmem_limit_bytes=56 * 2**20),
        cost_estimate=pl.CostEstimate(
            flops=2 * entries * LANES * LANES, bytes_accessed=entries * 1024, transcendentals=0
        ),
    )(near, own, imported, translations, *more_args)


def coarse_call(translations, near, own, imported, shift):
    class_count, boxes = near.shape
    no_source = own.shape[0] + imported.shape[0]
    more = -class_count % COARSE_GROUP
    near = jnp.pad(near, ((0, more), (0, 0)), constant_values=no_source)
    share = PIECE // boxes
    pieces = tuple(
        (c, share, c, share, c, range(c, c + share)) for c in range(0, COARSE_GROUP, share)
    )
    return translate(
        translations, near.reshape(-1, PIECE), own, imported, (shift,), pieces, COARSE_GROUP,
        class_count, True,
    )


def fine_call(translations, near, own, imported, codes, down):
    pieces = (
        (0, 1, 0, FINE_GROUP, None, ()),
        (1, 1, 0, 0, 0, ()),
        (2, 1, 0, 0, None, (0, 1)),
        (3, 1, 0, 0, None, (2, 3)),
    )
    (out,) = translate(
        translations, near, own, imported, (codes, down), pieces, FINE_GROUP, near.shape[0],
        False,
    )
    return out


def pack(own_rows, slots):
    places = lax.broadcasted_iota(jnp.int32, (slots.size, own_rows.shape[0]), 1)
    chosen = (slots.reshape(-1, 1) == places).astype(jnp.bfloat16)
    return jnp.dot(chosen, own_rows, preferred_element_type=jnp.float32).astype(jnp.bfloat16)


def on_device(
    multipoles_fine,
    multipoles_coarse,
    translations,
    shift_down,
    send_fine,
    send_coarse,
    near_fine,
    near_coarse,
    parent_fine,
    octant_fine,
    counts_coarse,
):
    coeffs, fine_boxes = multipoles_fine.shape
    coarse_boxes = multipoles_coarse.shape[1]
    extra = LANES - coeffs
    devices = send_fine.shape[1]

    own_coarse = jnp.pad(multipoles_coarse.T, ((0, 0), (0, extra)))
    own_fine = jnp.pad(multipoles_fine.T, ((0, 0), (0, extra)))

    def exchange(rows):
        return lax.all_to_all(rows, AXES, split_axis=0, concat_axis=0, tiled=True)

    imported_coarse = exchange(pack(own_coarse, send_coarse[0]))
    imported_fine = exchange(pack(own_fine, send_fine[0]))

    by_row = translations.transpose(1, 0, 2)
    local_coarse, down = coarse_call(
        by_row, near_coarse, own_coarse, imported_coarse, shift_down.transpose(1, 0, 2)
    )

    last_local = lax.dynamic_slice_in_dim(local_coarse, counts_coarse[0] - 1, 1, 1)
    route = [(i, i + 1) for i in range(devices - 1)]
    boundary = lax.ppermute(last_local, AXES, route)

    codes = jnp.where(
        parent_fine < coarse_boxes, octant_fine * coarse_boxes + parent_fine, 8 * coarse_boxes
    )
    local_fine = fine_call(by_row, near_fine, own_fine, imported_fine, codes, down)
    moved = jnp.sum(shift_down * boundary[:, 0], axis=2)
    octants = jnp.arange(8)[:, None]
    takes = (octants == octant_fine[:8]) & (parent_fine[:8] == coarse_boxes)
    first = jnp.sum(jnp.where(takes[:, None, :], moved[:, :, None], 0.0), axis=0)
    local_fine = lax.dynamic_update_slice(local_fine, local_fine[:, :8] + first, (0, 0))
    return (local_fine, local_coarse)


def solution(mesh):
    in_specs = (
        P(None, AXES),
        P(None, AXES),
        P(),
        P(),
        P(AXES, None, None),
        P(AXES, None, None),
        P(None, AXES),
        P(None, AXES),
        P(AXES),
        P(AXES),
        P(AXES),
    )
    out_specs = (P(None, AXES), P(None, AXES))
    return jax.shard_map(
        on_device, mesh=mesh, in_specs=in_specs, out_specs=out_specs, check_vma=False
    )
```

```python
import functools

import jax
import jax.numpy as jnp
from jax import lax
from jax.experimental import pallas as pl
from jax.experimental.pallas import tpu as pltpu
from jax.sharding import PartitionSpec as P

LANES = 128
PIECE = 1024
COARSE_GROUP = 32
FINE_GROUP = 4
AXES = ("gx", "gy")


def pick_tile(table, index_of, masks):
    tile = None
    for k in range(8):
        row = jnp.broadcast_to(table[pl.ds(index_of(k), 1), :], (8, LANES))
        tile = row if tile is None else jnp.where(masks[k], row, tile)
    return tile


def translate_kernel(*refs, pieces, group, last_classes, coarse, block=256):
    piece_count = len(pieces)
    near, own, imported, weights = refs[:4]
    if coarse:
        shift, out, down = refs[4:7]
    else:
        codes, down, first_rows, out = refs[4:8]
    refs = refs[7 if coarse else 8 :]
    table, gathered, total, spread, right, sems = refs[:6]
    buffers = refs[6:]
    step = pl.program_id(0)
    steps = pl.num_programs(0)
    own_count = own.shape[0]
    import_count = table.shape[0] - own_count - 8
    boxes = total.shape[0]
    coeffs, held, _ = weights.shape
    sublane = lax.broadcasted_iota(jnp.int32, (8, LANES), 0)
    masks = [sublane == k for k in range(8)]

    def fetch(at_step, part):
        return pltpu.make_async_copy(
            near.at[at_step * piece_count + part], buffers[part], sems.at[part]
        )

    @pl.when(step == 0)
    def _():
        for part in range(piece_count):
            fetch(0, part).start()
        gathered[...] = jnp.zeros_like(gathered)
        spread[...] = jnp.zeros_like(spread)
        right[...] = jnp.zeros_like(right)
        table[0:own_count, :] = jnp.zeros((own_count, LANES), jnp.float32)
        table[0:own_count, 0:coeffs] = own[...].astype(jnp.float32)

        table[own_count + import_count :, :] = jnp.zeros((8, LANES), jnp.float32)

        def widen(i, carry):
            first = pl.multiple_of(i * 128, 128)
            table[pl.ds(own_count + first, 128), :] = imported[pl.ds(first, 128), :].astype(
                jnp.float32
            )
            return carry

        lax.fori_loop(0, import_count // 128, widen, 0, unroll=2)
        if coarse:
            total[...] = jnp.zeros_like(total)
        else:

            def start_rows(i, carry):
                first = pl.multiple_of(i * 8, 8)
                total[pl.ds(first, 8), :] = pick_tile(down, lambda k: codes[first + k], masks)
                return carry

            lax.fori_loop(0, boxes // 8, start_rows, 0)
            total[0:8, :] += first_rows[...]

    offset = lax.rem(step, held // group) * group if held > group else 0

    def widen_matrices(source, first, count, classes):
        spread[first * 8 : (first + count) * 8, 0:coeffs] = (
            source[first : first + count, classes, :]
            .astype(jnp.float32)
            .reshape(count * 8, coeffs)
        )

    def arrange(c):
        rows = spread[pl.ds(offset + c % 8, LANES, stride=8), :]
        right[:, c * LANES : (c + 1) * LANES] = rows.astype(jnp.bfloat16)

    def multiply(first_row, rows, first_class, classes):
        span = pl.ds(first_class * LANES, classes * LANES)
        total[first_row : first_row + rows, :] += lax.dot_general(
            gathered[first_row : first_row + rows, span],
            right[:, span],
            (((1,), (1,)), ((), ())),
            preferred_element_type=jnp.float32,
        )

    for part, (first_class, classes, first_ready, ready, widened, arranged) in enumerate(pieces):
        extra = []
        if widened is not None:
            for first in range(0, coeffs, 8):
                extra.append(
                    functools.partial(
                        widen_matrices, weights, first, min(8, coeffs - first),
                        slice(widened, widened + 8),
                    )
                )
        for c in arranged:
            extra.append(functools.partial(arrange, c))
        tiles = classes * boxes // 16
        every = max(1, tiles // (len(extra) + 1))
        fetch(step, part).wait()
        buffer = buffers[part]
        done = 0
        for r in range(0, boxes, block):
            if ready:
                multiply(r, min(block, boxes), first_ready, ready)
            for c in range(classes):
                for v in range(r, min(r + block, boxes), 16):
                    halves = [
                        pick_tile(table, lambda k, at=c * boxes + v + h: buffer[at + k], masks)
                        for h in (0, 8)
                    ]
                    gathered[
                        v : v + 16, (first_class + c) * LANES : (first_class + c + 1) * LANES
                    ] = jnp.concatenate(halves, axis=0).astype(jnp.bfloat16)
                    done += 1
                    if extra and done % every == 0:
                        extra.pop(0)()
        for rest in extra:
            rest()
        fetch(jnp.minimum(step + 1, steps - 1), part).start()

    @pl.when(step == steps - 1)
    def _():
        for part in range(piece_count):
            fetch(step, part).wait()
        for r in range(0, boxes, 128):
            multiply(r, 128, 0, last_classes)
        out[...] = total[...].T[:coeffs, :]
        if coarse:
            widen_matrices(shift, 0, coeffs, slice(0, 8))
            for octant in range(8):
                down[octant * boxes : (octant + 1) * boxes, :] = lax.dot_general(
                    total[...],
                    spread[pl.ds(octant, LANES, stride=8), :],
                    (((1,), (1,)), ((), ())),
                    precision=lax.Precision.HIGHEST,
                    preferred_element_type=jnp.float32,
                )
            down[8 * boxes :, :] = jnp.zeros((8, LANES), jnp.float32)


def translate(translations, near, own, imported, more_args, pieces, group, class_count, coarse):
    coeffs = translations.shape[2]
    steps = near.shape[0] // len(pieces)
    boxes = PIECE // pieces[0][1]
    held = max(group, 8)
    shared = held // group
    whole = lambda t: (0, 0)
    in_specs = [
        pl.BlockSpec(near.shape, whole),
        pl.BlockSpec(own.shape, whole),
        pl.BlockSpec(imported.shape, whole),
        pl.BlockSpec((coeffs, held, coeffs), lambda t: (0, t // shared, 0)),
    ]
    out_specs = [pl.BlockSpec((coeffs, boxes), whole)]
    out_shape = [jax.ShapeDtypeStruct((coeffs, boxes), jnp.float32)]
    if coarse:
        in_specs.append(pl.BlockSpec(more_args[0].shape, lambda t: (0, 0, 0)))
        out_specs.append(pl.BlockSpec((8 * boxes + 8, LANES), whole))
        out_shape.append(jax.ShapeDtypeStruct((8 * boxes + 8, LANES), jnp.float32))
    else:
        in_specs.append(pl.BlockSpec(memory_space=pltpu.SMEM))
        in_specs += [pl.BlockSpec(more.shape, whole) for more in more_args[1:]]
    entries = steps * len(pieces) * PIECE
    return pl.pallas_call(
        functools.partial(
            translate_kernel,
            pieces=pieces,
            group=group,
            last_classes=class_count - (steps - 1) * group,
            coarse=coarse,
        ),
        grid=(steps,),
        in_specs=in_specs,
        out_specs=out_specs,
        out_shape=out_shape,
        scratch_shapes=[
            pltpu.VMEM((own.shape[0] + imported.shape[0] + 8, LANES), jnp.float32),
            pltpu.VMEM((boxes, group * LANES), jnp.bfloat16),
            pltpu.VMEM((boxes, LANES), jnp.float32),
            pltpu.VMEM((LANES * 8, LANES), jnp.float32),
            pltpu.VMEM((LANES, group * LANES), jnp.bfloat16),
            pltpu.SemaphoreType.DMA((len(pieces),)),
        ]
        + [pltpu.SMEM((PIECE,), jnp.int32) for _ in pieces],
        compiler_params=pltpu.CompilerParams(vmem_limit_bytes=56 * 2**20),
        cost_estimate=pl.CostEstimate(
            flops=2 * entries * LANES * LANES, bytes_accessed=entries * 1024, transcendentals=0
        ),
    )(near, own, imported, translations, *more_args)


def coarse_call(translations, near, own, imported, shift):
    class_count, boxes = near.shape
    no_source = own.shape[0] + imported.shape[0]
    more = -class_count % COARSE_GROUP
    near = jnp.pad(near, ((0, more), (0, 0)), constant_values=no_source)
    share = PIECE // boxes
    pieces = tuple(
        (c, share, 0, 0 if c else COARSE_GROUP, c, range(c, c + share))
        for c in range(0, COARSE_GROUP, share)
    )
    return translate(
        translations, near.reshape(-1, PIECE), own, imported, (shift,), pieces, COARSE_GROUP,
        class_count, True,
    )


def fine_call(translations, near, own, imported, codes, down, first_rows):
    pieces = (
        (0, 1, 0, FINE_GROUP, None, ()),
        (1, 1, 0, 0, 0, ()),
        (2, 1, 0, 0, None, (0, 1)),
        (3, 1, 0, 0, None, (2, 3)),
    )
    (out,) = translate(
        translations, near, own, imported, (codes, down, first_rows), pieces, FINE_GROUP,
        near.shape[0], False,
    )
    return out


def pack(own_rows, slots):
    places = lax.broadcasted_iota(jnp.int32, (slots.size, own_rows.shape[0]), 1)
    chosen = (slots.reshape(-1, 1) == places).astype(jnp.bfloat16)
    return jnp.dot(chosen, own_rows, preferred_element_type=jnp.float32).astype(jnp.bfloat16)


def on_device(
    multipoles_fine,
    multipoles_coarse,
    translations,
    shift_down,
    send_fine,
    send_coarse,
    near_fine,
    near_coarse,
    parent_fine,
    octant_fine,
    counts_coarse,
):
    coeffs, fine_boxes = multipoles_fine.shape
    coarse_boxes = multipoles_coarse.shape[1]
    extra = LANES - coeffs
    devices = send_fine.shape[1]

    own_coarse = jnp.pad(multipoles_coarse.T, ((0, 0), (0, extra)))
    own_fine = jnp.pad(multipoles_fine.T, ((0, 0), (0, extra)))

    def exchange(rows):
        return lax.all_to_all(rows, AXES, split_axis=0, concat_axis=0, tiled=True)

    imported_coarse = exchange(pack(own_coarse, send_coarse[0]))
    imported_fine = exchange(pack(own_fine, send_fine[0]))

    by_row = translations.transpose(1, 0, 2)
    local_coarse, down = coarse_call(
        by_row, near_coarse, multipoles_coarse.T, imported_coarse, shift_down.transpose(1, 0, 2)
    )

    last_local = lax.dynamic_slice_in_dim(local_coarse, counts_coarse[0] - 1, 1, 1)
    route = [(i, i + 1) for i in range(devices - 1)]
    boundary = lax.ppermute(last_local, AXES, route)

    codes = jnp.where(
        parent_fine < coarse_boxes, octant_fine * coarse_boxes + parent_fine, 8 * coarse_boxes
    )
    moved = jnp.sum(shift_down * boundary[:, 0], axis=2)
    takes = (jnp.arange(8) == octant_fine[:8, None]) & (parent_fine[:8, None] == coarse_boxes)
    first_rows = jnp.sum(jnp.where(takes[:, :, None], moved[None], 0.0), axis=1)
    first_rows = jnp.pad(first_rows, ((0, 0), (0, extra)))
    local_fine = fine_call(
        by_row, near_fine, multipoles_fine.T, imported_fine, codes, down, first_rows
    )
    return (local_fine, local_coarse)


def solution(mesh):
    in_specs = (
        P(None, AXES),
        P(None, AXES),
        P(),
        P(),
        P(AXES, None, None),
        P(AXES, None, None),
        P(None, AXES),
        P(None, AXES),
        P(AXES),
        P(AXES),
        P(AXES),
    )
    out_specs = (P(None, AXES), P(None, AXES))
    return jax.shard_map(
        on_device, mesh=mesh, in_specs=in_specs, out_specs=out_specs, check_vma=False
    )
```

```python
import functools

import jax
import jax.numpy as jnp
from jax import lax
from jax.experimental import pallas as pl
from jax.experimental.pallas import tpu as pltpu
from jax.sharding import PartitionSpec as P

LANES = 128
PIECE = 1024
COARSE_GROUP = 32
FINE_GROUP = 4
AXES = ("gx", "gy")


def pick_tile(table, index_of, masks):
    tile = None
    for k in range(8):
        row = jnp.broadcast_to(table[pl.ds(index_of(k), 1), :], (8, LANES))
        tile = row if tile is None else jnp.where(masks[k], row, tile)
    return tile


def translate_kernel(*refs, pieces, group, last_classes, coarse, block=512):
    piece_count = len(pieces)
    near, own, imported, weights = refs[:4]
    if coarse:
        shift, out, down = refs[4:7]
    else:
        codes, down, first_rows, out = refs[4:8]
    refs = refs[7 if coarse else 8 :]
    table, gathered, total, spread, right, sems = refs[:6]
    buffers = refs[6:]
    step = pl.program_id(0)
    steps = pl.num_programs(0)
    own_count = own.shape[0]
    import_count = table.shape[0] - own_count - 8
    boxes = total.shape[0]
    coeffs, held, _ = weights.shape
    sublane = lax.broadcasted_iota(jnp.int32, (8, LANES), 0)
    masks = [sublane == k for k in range(8)]

    def fetch(at_step, part):
        return pltpu.make_async_copy(
            near.at[at_step * piece_count + part], buffers[part], sems.at[part]
        )

    @pl.when(step == 0)
    def _():
        for part in range(piece_count):
            fetch(0, part).start()
        gathered[...] = jnp.zeros_like(gathered)
        spread[...] = jnp.zeros_like(spread)
        right[...] = jnp.zeros_like(right)
        table[0:own_count, :] = jnp.zeros((own_count, LANES), jnp.float32)
        table[0:own_count, 0:coeffs] = own[...].astype(jnp.float32)

        table[own_count + import_count :, :] = jnp.zeros((8, LANES), jnp.float32)

        def widen(i, carry):
            first = pl.multiple_of(i * 128, 128)
            table[pl.ds(own_count + first, 128), :] = imported[pl.ds(first, 128), :].astype(
                jnp.float32
            )
            return carry

        lax.fori_loop(0, import_count // 128, widen, 0, unroll=2)
        if coarse:
            total[...] = jnp.zeros_like(total)
        else:

            def start_rows(i, carry):
                first = pl.multiple_of(i * 8, 8)
                total[pl.ds(first, 8), :] = pick_tile(down, lambda k: codes[first + k], masks)
                return carry

            lax.fori_loop(0, boxes // 8, start_rows, 0)
            total[0:8, :] += first_rows[...]

    offset = lax.rem(step, held // group) * group if held > group else 0

    def widen_matrices(source, first, count, classes):
        spread[first * 8 : (first + count) * 8, 0:coeffs] = (
            source[first : first + count, classes, :]
            .astype(jnp.float32)
            .reshape(count * 8, coeffs)
        )

    def arrange(c):
        rows = spread[pl.ds(offset + c % 8, LANES, stride=8), :]
        span = slice(c * LANES, (c + 1) * LANES)
        if coarse:
            right[:, span] = rows.astype(jnp.bfloat16)
        else:
            right[span, :] = rows.T.astype(jnp.bfloat16)

    def multiply(first_row, rows, first_class, classes):
        span = pl.ds(first_class * LANES, classes * LANES)
        total[first_row : first_row + rows, :] += lax.dot_general(
            gathered[first_row : first_row + rows, span],
            right[:, span] if coarse else right[span, :],
            (((1,), (1 if coarse else 0,)), ((), ())),
            preferred_element_type=jnp.float32,
        )

    for part, (first_class, classes, first_ready, ready, widened, arranged) in enumerate(pieces):
        extra = []
        if widened is not None:
            for first in range(0, coeffs, 8):
                extra.append(
                    functools.partial(
                        widen_matrices, weights, first, min(8, coeffs - first),
                        slice(widened, widened + 8),
                    )
                )
        for c in arranged:
            extra.append(functools.partial(arrange, c))
        tiles = classes * boxes // 16
        every = max(1, tiles // (len(extra) + 1))
        fetch(step, part).wait()
        buffer = buffers[part]
        done = 0
        for r in range(0, boxes, block):
            if ready:
                multiply(r, min(block, boxes), first_ready, ready)
            for c in range(classes):
                for v in range(r, min(r + block, boxes), 16):
                    halves = [
                        pick_tile(table, lambda k, at=c * boxes + v + h: buffer[at + k], masks)
                        for h in (0, 8)
                    ]
                    gathered[
                        v : v + 16, (first_class + c) * LANES : (first_class + c + 1) * LANES
                    ] = jnp.concatenate(halves, axis=0).astype(jnp.bfloat16)
                    done += 1
                    if extra and done % every == 0:
                        extra.pop(0)()
        for rest in extra:
            rest()
        fetch(jnp.minimum(step + 1, steps - 1), part).start()

    @pl.when(step == steps - 1)
    def _():
        for part in range(piece_count):
            fetch(step, part).wait()
        for r in range(0, boxes, 128):
            multiply(r, 128, 0, last_classes)
        out[...] = total[...].T[:coeffs, :]
        if coarse:
            widen_matrices(shift, 0, coeffs, slice(0, 8))
            for octant in range(8):
                down[octant * boxes : (octant + 1) * boxes, :] = lax.dot_general(
                    total[...],
                    spread[pl.ds(octant, LANES, stride=8), :],
                    (((1,), (1,)), ((), ())),
                    precision=lax.Precision.HIGHEST,
                    preferred_element_type=jnp.float32,
                )
            down[8 * boxes :, :] = jnp.zeros((8, LANES), jnp.float32)


def translate(translations, near, own, imported, more_args, pieces, group, class_count, coarse):
    coeffs = translations.shape[2]
    steps = near.shape[0] // len(pieces)
    boxes = PIECE // pieces[0][1]
    held = max(group, 8)
    shared = held // group
    whole = lambda t: (0, 0)
    in_specs = [
        pl.BlockSpec(near.shape, whole),
        pl.BlockSpec(own.shape, whole),
        pl.BlockSpec(imported.shape, whole),
        pl.BlockSpec((coeffs, held, coeffs), lambda t: (0, t // shared, 0)),
    ]
    out_specs = [pl.BlockSpec((coeffs, boxes), whole)]
    out_shape = [jax.ShapeDtypeStruct((coeffs, boxes), jnp.float32)]
    if coarse:
        in_specs.append(pl.BlockSpec(more_args[0].shape, lambda t: (0, 0, 0)))
        out_specs.append(pl.BlockSpec((8 * boxes + 8, LANES), whole))
        out_shape.append(jax.ShapeDtypeStruct((8 * boxes + 8, LANES), jnp.float32))
    else:
        in_specs.append(pl.BlockSpec(memory_space=pltpu.SMEM))
        in_specs += [pl.BlockSpec(more.shape, whole) for more in more_args[1:]]
    entries = steps * len(pieces) * PIECE
    return pl.pallas_call(
        functools.partial(
            translate_kernel,
            pieces=pieces,
            group=group,
            last_classes=class_count - (steps - 1) * group,
            coarse=coarse,
        ),
        grid=(steps,),
        in_specs=in_specs,
        out_specs=out_specs,
        out_shape=out_shape,
        scratch_shapes=[
            pltpu.VMEM((own.shape[0] + imported.shape[0] + 8, LANES), jnp.float32),
            pltpu.VMEM((boxes, group * LANES), jnp.bfloat16),
            pltpu.VMEM((boxes, LANES), jnp.float32),
            pltpu.VMEM((LANES * 8, LANES), jnp.float32),
            pltpu.VMEM((LANES, group * LANES) if coarse else (group * LANES, LANES), jnp.bfloat16),
            pltpu.SemaphoreType.DMA((len(pieces),)),
        ]
        + [pltpu.SMEM((PIECE,), jnp.int32) for _ in pieces],
        compiler_params=pltpu.CompilerParams(vmem_limit_bytes=56 * 2**20),
        cost_estimate=pl.CostEstimate(
            flops=2 * entries * LANES * LANES, bytes_accessed=entries * 1024, transcendentals=0
        ),
    )(near, own, imported, translations, *more_args)


def coarse_call(translations, near, own, imported, shift):
    class_count, boxes = near.shape
    no_source = own.shape[0] + imported.shape[0]
    more = -class_count % COARSE_GROUP
    near = jnp.pad(near, ((0, more), (0, 0)), constant_values=no_source)
    share = PIECE // boxes
    pieces = tuple(
        (c, share, 0, 0 if c else COARSE_GROUP, c, range(c, c + share))
        for c in range(0, COARSE_GROUP, share)
    )
    return translate(
        translations, near.reshape(-1, PIECE), own, imported, (shift,), pieces, COARSE_GROUP,
        class_count, True,
    )


def fine_call(translations, near, own, imported, codes, down, first_rows):
    pieces = (
        (0, 1, 0, FINE_GROUP, None, ()),
        (1, 1, 0, 0, 0, ()),
        (2, 1, 0, 0, None, (0, 1)),
        (3, 1, 0, 0, None, (2, 3)),
    )
    (out,) = translate(
        translations, near, own, imported, (codes, down, first_rows), pieces, FINE_GROUP,
        near.shape[0], False,
    )
    return out


def pack(own_rows, slots):
    places = lax.broadcasted_iota(jnp.int32, (slots.size, own_rows.shape[0]), 1)
    chosen = (slots.reshape(-1, 1) == places).astype(jnp.bfloat16)
    return jnp.dot(chosen, own_rows, preferred_element_type=jnp.float32).astype(jnp.bfloat16)


def on_device(
    multipoles_fine,
    multipoles_coarse,
    translations,
    shift_down,
    send_fine,
    send_coarse,
    near_fine,
    near_coarse,
    parent_fine,
    octant_fine,
    counts_coarse,
):
    coeffs, fine_boxes = multipoles_fine.shape
    coarse_boxes = multipoles_coarse.shape[1]
    extra = LANES - coeffs
    devices = send_fine.shape[1]

    own_coarse = jnp.pad(multipoles_coarse.T, ((0, 0), (0, extra)))
    own_fine = jnp.pad(multipoles_fine.T, ((0, 0), (0, extra)))

    def exchange(rows):
        return lax.all_to_all(rows, AXES, split_axis=0, concat_axis=0, tiled=True)

    imported_coarse = exchange(pack(own_coarse, send_coarse[0]))
    imported_fine = exchange(pack(own_fine, send_fine[0]))

    by_row = translations.transpose(1, 0, 2)
    local_coarse, down = coarse_call(
        by_row, near_coarse, multipoles_coarse.T, imported_coarse, shift_down.transpose(1, 0, 2)
    )

    last_local = lax.dynamic_slice_in_dim(local_coarse, counts_coarse[0] - 1, 1, 1)
    route = [(i, i + 1) for i in range(devices - 1)]
    boundary = lax.ppermute(last_local, AXES, route)

    codes = jnp.where(
        parent_fine < coarse_boxes, octant_fine * coarse_boxes + parent_fine, 8 * coarse_boxes
    )
    moved = jnp.sum(shift_down * boundary[:, 0], axis=2)
    takes = (jnp.arange(8) == octant_fine[:8, None]) & (parent_fine[:8, None] == coarse_boxes)
    first_rows = jnp.sum(jnp.where(takes[:, :, None], moved[None], 0.0), axis=1)
    first_rows = jnp.pad(first_rows, ((0, 0), (0, extra)))
    local_fine = fine_call(
        by_row, near_fine, multipoles_fine.T, imported_fine, codes, down, first_rows
    )
    return (local_fine, local_coarse)


def solution(mesh):
    in_specs = (
        P(None, AXES),
        P(None, AXES),
        P(),
        P(),
        P(AXES, None, None),
        P(AXES, None, None),
        P(None, AXES),
        P(None, AXES),
        P(AXES),
        P(AXES),
        P(AXES),
    )
    out_specs = (P(None, AXES), P(None, AXES))
    return jax.shard_map(
        on_device, mesh=mesh, in_specs=in_specs, out_specs=out_specs, check_vma=False
    )
```
